128 devices in a mesh: row: 8 (over z_hi, x), col: 16 (over z_lo, y, core).
Axes of the slice: x: 4, y: 4, z: 4 (z_hi: 2, z_lo: 2; z = z_hi * 2 + z_lo), core: 2. Of those that a mesh axis runs over, the one named last changes fastest.
Arguments:
- environment: float32 [2, 2048, 4096], P(None, 'row', 'col'), may hold values from -6 to 6
- initial_site: float32 [2, 2, 4096, 4096], P(None, None, 'col', 'row'), may hold values from -0.09375 to 0.09375
- compressed_site: float32 [2, 2, 2048, 2048], P(None, None, 'col', 'row'), may hold values from -0.09375 to 0.09375
Outputs:
- new_environment: float32 [2, 2048, 4096], P(None, 'row', 'col')
The draws below stay inside these ranges and needn't reach their ends.
All inputs are finite; a program needn't handle non-finite values.
Results may differ from the reference program's by a relative error of at most 0.0001.
Values sent between devices are 32-bit elements; how exact they have to be, the bound alone decides.
No kernel may reach another device: no remote copies, remote signals or barrier semaphores. Data moves between devices by JAX's collectives and lax.ppermute only.
A program may use at most 128 MiB of HBM per device.

```python
import jax
import jax.numpy as jnp
from jax import lax

NF = 2
DB = 2048
DA = 4096


def spiked(values, rng, source, target, parts, factor):
    def block_of(dim):
        return (jnp.arange(values.shape[dim]) // (values.shape[dim] // parts)).reshape((-1,) + (1,) * (values.ndim - 1 - dim))

    one_side = jax.random.permutation(rng, parts)[block_of(target)]
    far = (block_of(target) + parts // 2) % parts
    return jnp.where((block_of(source) == one_side) | (block_of(source) == far), factor * values, values)


def block_levels(key, shape, cuts, least, top_value):
    def one(axis_at, blocks):
        heights = jax.random.uniform(jax.random.fold_in(jax.random.fold_in(key, 6), axis_at), (blocks,), jnp.float32, least / len(cuts), top_value / len(cuts))
        return jnp.repeat(jnp.exp(heights), shape[axis_at] // blocks).reshape((-1,) + (1,) * (len(shape) - axis_at - 1))

    loudness = one(*cuts[0])
    for cut in cuts[1:]:
        loudness = loudness * one(*cut)
    return loudness


def centred(key, shape, deviation, reach, pieces=(), kind=jnp.bfloat16):
    array = jax.random.normal(key, shape, jnp.float32) * deviation
    if len(pieces) > 0:
        array = block_levels(key, shape, pieces, -0.22, 0.18) * array
    return jnp.clip(array, min=-reach, max=reach).astype(kind)


def gaussian_with(stream_key, dims, scale, reach, shards, heavy, held_as=jnp.bfloat16):
    entries = scale * jax.random.normal(stream_key, dims, jnp.float32)
    if shards:
        entries = entries * block_levels(stream_key, dims, shards, -0.22, 0.18)
    return jnp.clip(spiked(entries, jax.random.fold_in(stream_key, 3), *heavy), -reach, reach).astype(held_as)


def setup_inputs(seed: int = 0) -> dict:
    streams_of = jax.random.split(jax.random.key(seed), 4)
    environment = centred(streams_of[0], (2, DB, DA), 1.0, 6.0, ((1, 8), (2, 16)), jnp.float32)
    initial_site = gaussian_with(streams_of[1], (NF, 2, DA, DA), (2 * DA) ** -0.5, 0.09375, ((2, 16), (3, 8)), (2, 3, 16, 2.0), jnp.float32)
    compressed_site = centred(streams_of[2], (NF, 2, DB, DB), (2 * DB) ** -0.5, 0.09375, ((2, 16), (3, 8)), jnp.float32)
    return dict(environment=environment, initial_site=initial_site, compressed_site=compressed_site)


def matmul(left, right):
    return jnp.dot(left, right, precision=lax.Precision.HIGHEST, preferred_element_type=jnp.float32)


def reference(environment, initial_site, compressed_site):
    env_re = environment[0]
    env_im = environment[1]
    total_re = jnp.zeros((DB, DA), jnp.float32)
    total_im = jnp.zeros((DB, DA), jnp.float32)
    for level in range(NF):
        comp_re = compressed_site[level, 0].T
        comp_im = compressed_site[level, 1].T
        mixed_re = matmul(comp_re, env_re) + matmul(comp_im, env_im)
        mixed_im = matmul(comp_re, env_im) - matmul(comp_im, env_re)
        orig_re = initial_site[level, 0]
        orig_im = initial_site[level, 1]
        total_re = total_re + matmul(mixed_re, orig_re) - matmul(mixed_im, orig_im)
        total_im = total_im + matmul(mixed_re, orig_im) + matmul(mixed_im, orig_re)
    return jnp.stack([total_re, total_im])
```

```python
import jax
import jax.numpy as jnp
from jax import lax
from jax.experimental import pallas as pl
from jax.experimental.pallas import tpu as pltpu
from jax.sharding import Mesh, PartitionSpec as P

PARTS = {"zh": 2, "x": 4, "zl": 2, "y": 4, "core": 2}
F32 = jnp.float32
BF16 = jnp.bfloat16


def move(value, axis, step):
    n = PARTS[axis]
    return lax.ppermute(value, axis, [(i, (i + step) % n) for i in range(n)])


def split(value):
    high = value.astype(BF16)
    return high, (value - high.astype(F32)).astype(BF16)


def dot3(left, right, dims):
    (lh, ll), (rh, rl) = left, right

    def one(a, b):
        return lax.dot_general(a, b, (dims, ((), ())), preferred_element_type=F32)

    return one(lh, rh) + (one(lh, rl) + one(ll, rh))


def mixed_kernel(place, b_ref, *refs):
    l_refs, out_ref = refs[:-1], refs[-1]
    depth = l_refs[0].shape[1]
    for level in range(2):
        total = [None, None]
        for pair in range(len(l_refs) // 2):
            rows = [pl.multiple_of(place[2 * pair + i] * depth, depth) for i in range(2)]

            def block(part):
                return split(
                    jnp.concatenate([b_ref[level, part, pl.ds(r, depth), :] for r in rows], axis=0)
                )

            def env(part):
                return split(
                    jnp.concatenate([l_refs[2 * pair + i][part] for i in range(2)], axis=0)
                )

            b_re, b_im, l_re, l_im = block(0), block(1), env(0), env(1)
            dims = ((0,), (0,))
            new = [
                dot3(b_re, l_re, dims) + dot3(b_im, l_im, dims),
                dot3(b_re, l_im, dims) - dot3(b_im, l_re, dims),
            ]
            total = new if total[0] is None else [t + u for t, u in zip(total, new)]
        for part in range(2):
            out_ref[level, part] = total[part]


def update_kernel(place, m_ref, *refs):
    a_refs, out_ref = refs[:-1], refs[-1]
    wide = a_refs[0].shape[-1]
    dims = ((1,), (0,))
    left = [[split(m_ref[level, part]) for part in range(2)] for level in range(2)]
    for j in range(4):
        total = None
        for level in range(2):
            if j < 3:
                a_re, a_im = a_refs[j][level, 0], a_refs[j][level, 1]
            else:
                a_re, a_im = a_refs[3 + level][0], a_refs[3 + level][1]
            (rh, rl), (ih, il) = split(a_re), split(a_im)

            def beside(p, q):
                return jnp.concatenate([p, q], axis=1)

            new = dot3(left[level][0], (beside(rh, ih), beside(rl, il)), dims) + dot3(
                left[level][1], (beside(-ih, rh), beside(-il, rl)), dims
            )
            total = new if total is None else total + new
        out_ref[place[j], 0] = total[:, :wide]
        out_ref[place[j], 1] = total[:, wide:]


def call(kernel, out_shape, flops, place, *operands):
    vmem = pl.BlockSpec(memory_space=pltpu.VMEM)
    size = sum(4 * v.size for v in operands) + 4 * out_shape.size
    return pl.pallas_call(
        kernel,
        out_shape=out_shape,
        in_specs=[pl.BlockSpec(memory_space=pltpu.SMEM)] + [vmem] * len(operands),
        out_specs=vmem,
        compiler_params=pltpu.CompilerParams(vmem_limit_bytes=48 * 1024 * 1024),
        cost_estimate=pl.CostEstimate(flops=flops, bytes_accessed=size, transcendentals=0),
    )(place, *operands)


def mixed_partial(place, site, blocks):
    levels, _, _, b = site.shape
    a = blocks[0].shape[-1]
    out = jax.ShapeDtypeStruct((levels, 2, b, a), F32)
    flops = 2 * 3 * 4 * levels * site.shape[2] * b * a
    return call(mixed_kernel, out, flops, place, site, *blocks)


def update_partial(place, mixed, pieces):
    levels, _, b, a = mixed.shape
    c = pieces[0].shape[-1]
    out = jax.ShapeDtypeStruct((4, 2, b, c), F32)
    flops = 2 * 3 * 4 * levels * b * a * 4 * c
    return call(update_kernel, out, flops, place, mixed, *pieces)


def half(value, index, axis):
    size = value.shape[axis] // 2
    return lax.dynamic_slice_in_dim(value, index * size, size, axis)


def reduce_y(parts):
    up = move(parts[2, 0], "y", 1)
    down = move(parts[2, 1], "y", -1)
    up = move(jnp.stack([parts[1, 0] + up, parts[1, 1]]), "y", 1)
    down = move(jnp.stack([parts[3, 0], parts[3, 1] + down]), "y", -1)
    return parts[0] + up + down


def local(environment, initial_site, compressed_site):
    zh, x, zl, y, core = (lax.axis_index(name) for name in PARTS)

    rows_mine = half(environment, core, 1)
    rows_other = move(half(environment, 1 - core, 1), "core", 1)
    env = jnp.concatenate([rows_mine, rows_other], axis=2)
    cols_mine = half(initial_site, core, 3)
    cols_other = move(half(initial_site, 1 - core, 3), "core", 1)
    site = jnp.concatenate([cols_mine, cols_other], axis=2)

    comp = lax.all_gather(compressed_site, ("zl", "y"), axis=2, tiled=True)

    env_1 = move(env, "x", -1)
    env_3 = move(env, "x", 1)
    far_0 = move(env, "zh", 1)
    env_2 = jnp.stack([move(env_1[0], "x", -1), move(env_3[1], "x", 1)])
    far_1 = move(env_1, "zh", 1)
    far_3 = move(env_3, "zh", 1)
    far_2 = move(env_2, "zh", 1)
    blocks = [env, env_1, env_2, env_3, far_0, far_1, far_2, far_3]
    place = jnp.stack(
        [(zh if i < 4 else 1 - zh) * 4 + (x + i) % 4 for i in range(8)]
    ).astype(jnp.int32)

    share = mixed_partial(place, comp, blocks)
    other = move(share, "core", 1)
    wide = share.shape[-1] // 2
    mixed_mine = share[..., :wide] + other[..., wide:]
    mixed = jnp.concatenate([mixed_mine, share[..., wide:] + other[..., :wide]], axis=-1)
    far_mine = move(mixed_mine, "zh", 1)
    mixed_far = jnp.concatenate([far_mine, move(far_mine, "core", 1)], axis=-1)

    slices = []
    width = site.shape[-1] // 2
    for s in range(2):
        a_0 = site[..., s * width : (s + 1) * width]
        a_1 = move(a_0, "x", -1)
        a_3 = move(a_0, "x", 1)
        a_2 = [move(a_1[0], "x", -1), move(a_3[1], "x", 1)]
        slices.append([a_0, a_1, a_3, *a_2])
    order = jnp.stack([(x + j - y) % 4 for j in (0, 1, 3, 2)]).astype(jnp.int32)

    results = []
    for s in range(2):
        mine = reduce_y(update_partial(order, mixed, slices[s]))
        far = reduce_y(update_partial(order, mixed_far, slices[s]))
        same = zl == zh
        got = move(jnp.where(same, far, mine), "zl", 1)
        full = jnp.where(same, mine, far) + got
        results.append(lax.ppermute(full, ("zh", "zl"), [(0, 0), (1, 2), (2, 1), (3, 3)]))
    return jnp.concatenate(results, axis=2)


def solution(mesh):
    names = tuple(PARTS)
    parts = Mesh(mesh.devices.reshape(tuple(PARTS.values())), names)
    row, col = names[:2], names[2:]
    return jax.shard_map(
        local,
        mesh=parts,
        in_specs=(P(None, row, col), P(None, None, col, row), P(None, None, col, row)),
        out_specs=P(None, row, col),
        check_vma=False,
    )
```

```python
import functools

import jax
import jax.numpy as jnp
from jax import lax
from jax.experimental import pallas as pl
from jax.experimental.pallas import tpu as pltpu
from jax.sharding import Mesh, PartitionSpec as P

PARTS = {"zh": 2, "x": 4, "zl": 2, "y": 4, "core": 2}
F32 = jnp.float32
BF16 = jnp.bfloat16
COST = 0.02
MIXED_COST = 0.02
VMEM = 24 * 1024 * 1024
MIXED_VMEM = 40 * 1024 * 1024


def move(value, axis, step):
    n = PARTS[axis]
    return lax.ppermute(value, axis, [(i, (i + step) % n) for i in range(n)])


def split(value):
    high = value.astype(BF16)
    return high, (value - high.astype(F32)).astype(BF16)


def dot3(left, right, dims):
    (lh, ll), (rh, rl) = left, right

    def one(a, b):
        return lax.dot_general(a, b, (dims, ((), ())), preferred_element_type=F32)

    return one(lh, rh) + (one(lh, rl) + one(ll, rh))


def mixed_kernel(e_0, e_1, e_3, e_2low, e_2high, b_ref, out_ref, l_hi, l_lo):
    zh, x = lax.axis_index("zh"), lax.axis_index("x")
    depth = e_0.shape[2]

    @pl.when((pl.program_id(0) == 0) & (pl.program_id(1) == 0))
    def _():
        for far in range(2):
            for j in range(4):
                row = 4 * lax.rem(zh + far, 2) + lax.rem(x + j, 4)
                at = pl.ds(pl.multiple_of(row * depth, depth), depth)
                if j == 2:
                    ref, index = (e_2low, e_2high)[far], ()
                else:
                    ref, index = (e_0, e_1, None, e_3)[j], (far,)
                re, im = ref[(*index, 0)], ref[(*index, 1)]
                for part, block in enumerate((re, im, re + im)):
                    l_hi[part, at, :], l_lo[part, at, :] = split(block)

    dims = ((0,), (0,))
    l_re, l_im, l_sum = [(l_hi[part], l_lo[part]) for part in range(3)]
    re, im = [jnp.concatenate([b_ref[r, 0, part] for r in range(8)], axis=0) for part in range(2)]
    first, second = dot3(split(re), l_re, dims), dot3(split(im), l_im, dims)
    out_ref[0, 0] = first + second
    out_ref[0, 1] = dot3(split(re - im), l_sum, dims) - first + second


def update_kernel(own, other, *refs):
    x, y, zh = (lax.axis_index(name) for name in ("x", "y", "zh"))
    a_refs, (out_ref, m_hi, m_lo) = refs[:-3], refs[-3:]
    b, a = own.shape[2:]
    wide = a_refs[0].shape[-1]
    dims = ((1,), (0,))

    for level in range(2):
        for part in range(2):
            turned = other[level, part]
            turned = jnp.concatenate([turned[:, a // 2 :], turned[:, : a // 2]], axis=1)
            m_hi[level, part], m_lo[level, part] = split(own[level, part] + turned)

    def beside(p, q):
        return jnp.concatenate([p, q], axis=1)

    for j in range(4):
        sides = []
        for level in range(2):
            (rh, rl), (ih, il) = [
                split(jnp.concatenate([ref[level, part] for ref in a_refs[2 * j : 2 * j + 2]], axis=0))
                for part in range(2)
            ]
            sides.append(((beside(rh, ih), beside(rl, il)), (beside(-ih, rh), beside(-il, rl))))
        at = lax.rem(x + j + 4 - y, 4)
        for half_at in range(2):
            rows = slice(half_at * (b // 2), (half_at + 1) * (b // 2))
            total = None
            for level in range(2):
                for part in range(2):
                    left = m_hi[level, part, rows, :], m_lo[level, part, rows, :]
                    new = dot3(left, sides[level][part], dims)
                    total = new if total is None else total + new
            to = lax.rem(half_at + zh, 2)
            out_ref[at, to, 0] = total[:, :wide]
            out_ref[at, to, 1] = total[:, wide:]


def cost(flops, *values, scale=1):
    size = sum(v.dtype.itemsize * v.size for v in values)
    return pl.CostEstimate(flops=int(scale * flops), bytes_accessed=size, transcendentals=0)


def whole(n):
    return [pl.BlockSpec(memory_space=pltpu.VMEM)] * n


def mixed_partial(envs, sites):
    _, levels, _, depth, b = sites.shape
    a = envs[0].shape[-1]
    out = jax.ShapeDtypeStruct((levels, 2, 2 * b, a), F32)
    return pl.pallas_call(
        mixed_kernel,
        grid=(levels, 2),
        out_shape=out,
        in_specs=whole(len(envs))
        + [pl.BlockSpec((8, 1, 2, depth, b), lambda level, i: (i, level, 0, 0, 0))],
        out_specs=pl.BlockSpec((1, 2, b, a), lambda level, i: (level, 0, i, 0)),
        scratch_shapes=[pltpu.VMEM((3, 8 * depth, a), BF16)] * 2,
        compiler_params=pltpu.CompilerParams(vmem_limit_bytes=MIXED_VMEM),
        cost_estimate=cost(2 * 3 * 3 * levels * 8 * depth * 2 * b * a, out, sites, scale=MIXED_COST),
    )(*envs, sites)


def update_partial(shares, sites):
    levels, _, b, a = shares[0].shape
    c = sites[0].shape[-1]
    out = jax.ShapeDtypeStruct((4, 2, 2, b // 2, c), F32)
    operands = (*shares, *sites)
    return pl.pallas_call(
        update_kernel,
        out_shape=out,
        in_specs=whole(len(operands)),
        out_specs=pl.BlockSpec(memory_space=pltpu.VMEM),
        scratch_shapes=[pltpu.VMEM((levels, 2, b, a), BF16)] * 2,
        compiler_params=pltpu.CompilerParams(vmem_limit_bytes=VMEM),
        cost_estimate=cost(2 * 3 * 4 * levels * b * a * 4 * c, out, *operands, scale=COST),
    )(*operands)


def half(value, index, axis):
    size = value.shape[axis] // 2
    return lax.dynamic_slice_in_dim(value, index * size, size, axis)


def first_step(parts):
    return [move(parts[2, 0], "y", 1), move(parts[2, 1], "y", -1)]


def second_step(parts, came):
    up = move(jnp.stack([parts[1, 0] + came[0], parts[1, 1]]), "y", 1)
    down = move(jnp.stack([parts[3, 0], parts[3, 1] + came[1]]), "y", -1)
    return [up, down]


def to_place(mine, far, same):
    axes = ("zh", "zl")
    near = lax.ppermute(far, axes, [(1, 2), (2, 1)])
    got = lax.ppermute(jnp.where(same, far, mine), axes, [(0, 2), (1, 0), (2, 3), (3, 1)])
    return jnp.where(same, mine, near) + got


def local(environment, initial_site, compressed_site):
    zh, x, zl, y, core = (lax.axis_index(name) for name in PARTS)
    tie = lax.optimization_barrier

    comp = lax.all_gather(compressed_site, ("zh", "zl", "y"), axis=0)

    rows_other = move(half(environment, 1 - core, 1), "core", 1)
    env = jnp.concatenate([half(environment, core, 1), rows_other], axis=2)
    width = initial_site.shape[3] // 4
    cols_mine = half(initial_site, core, 3)
    cols_other = move(half(initial_site, 1 - core, 3), "core", 1)
    p_0, q_0 = [
        [v[..., i * width : (i + 1) * width] for v in (cols_mine, cols_other)] for i in range(2)
    ]

    env_far = move(env, "zh", 1)
    p_1 = [move(v, "x", -1) for v in p_0]
    p_3 = [move(v, "x", 1) for v in p_0]
    env, env_far, *more = tie((env, env_far, *p_1, *p_3, *q_0))
    p_1, p_3, q_0 = more[:2], more[2:4], more[4:]
    e_0 = jnp.stack([env, env_far])
    e_1 = move(e_0, "x", -1)
    e_3 = move(e_0, "x", 1)
    e_1, e_3, *more = tie((e_1, e_3, *p_1, *p_3))
    p_1, p_3 = more[:2], more[2:]
    e_2low = move(e_1[0], "x", -1)
    e_2high = move(e_3[1], "x", 1)
    p_2 = [move(p_1[0], "x", -1), move(p_3[1], "x", 1)]
    e_2low, e_2high, *more = tie((e_2low, e_2high, *p_2, *q_0))
    p_2, q_0 = more[:2], more[2:]
    q_own = [move(q_0[0], "x", -1), move(q_0[0], "x", 1)]

    share = mixed_partial([e_0, e_1, e_3, e_2low, e_2high], comp)
    share, *more = tie((share, *q_own, *q_0))
    q_own, q_0 = more[:2], more[2:]
    other = move(share, "core", 1)
    q_other = [move(q_0[1], "x", -1), move(q_0[1], "x", 1)]

    parts_0 = update_partial([share, other], [*p_0, *p_1, *p_2, *p_3])
    parts_0, *more = tie((parts_0, *q_own, *q_other))
    q_own, q_other = more[:2], more[2:]
    q_1, q_3 = zip(q_own, q_other)
    q_2 = [move(q_own[0], "x", -1), move(q_other[1], "x", 1)]
    came_0 = first_step(parts_0)
    *q_2, up, down = tie((*q_2, *came_0))
    came_0 = [up, down]
    came_0 = second_step(parts_0, came_0)
    parts_1 = update_partial([share, other], [*q_0, *q_1, *q_2, *q_3])
    came_1 = first_step(parts_1)
    parts_1, *came = tie((parts_1, *came_0, *came_1))
    came_0, came_1 = came[:2], came[2:]
    came_1 = second_step(parts_1, came_1)

    results = []
    for parts, came in ((parts_0, came_0), (parts_1, came_1)):
        mine, far = parts[0] + came[0] + came[1]
        results.append(to_place(mine, far, zl == zh))
    return jnp.concatenate(results, axis=2)


def solution(mesh):
    names = tuple(PARTS)
    parts = Mesh(mesh.devices.reshape(tuple(PARTS.values())), names)
    row, col = names[:2], names[2:]
    return jax.shard_map(
        local,
        mesh=parts,
        in_specs=(P(None, row, col), P(None, None, col, row), P(None, None, col, row)),
        out_specs=P(None, row, col),
        check_vma=False,
    )
```

```python
import functools

import jax
import jax.numpy as jnp
from jax import lax
from jax.experimental import pallas as pl
from jax.experimental.pallas import tpu as pltpu
from jax.sharding import Mesh, PartitionSpec as P

PARTS = {"zh": 2, "x": 4, "zl": 2, "y": 4, "core": 2}
F32 = jnp.float32
BF16 = jnp.bfloat16
COST = 0.02
MIXED_COST = 0.02
VMEM = 24 * 1024 * 1024
MIXED_VMEM = 40 * 1024 * 1024


def move(value, axis, step):
    n = PARTS[axis]
    return lax.ppermute(value, axis, [(i, (i + step) % n) for i in range(n)])


def split(value):
    high = value.astype(BF16)
    return high, (value - high.astype(F32)).astype(BF16)


def dot3(left, right, dims):
    (lh, ll), (rh, rl) = left, right

    def one(a, b):
        return lax.dot_general(a, b, (dims, ((), ())), preferred_element_type=F32)

    return one(lh, rh) + (one(lh, rl) + one(ll, rh))


def mixed_kernel(e_0, e_1, e_3, e_2low, e_2high, b_ref, out_ref, l_hi, l_lo):
    zh, x = lax.axis_index("zh"), lax.axis_index("x")
    depth = e_0.shape[2]

    @pl.when((pl.program_id(0) == 0) & (pl.program_id(1) == 0))
    def _():
        for far in range(2):
            for j in range(4):
                row = 4 * lax.rem(zh + far, 2) + lax.rem(x + j, 4)
                at = pl.ds(pl.multiple_of(row * depth, depth), depth)
                if j == 2:
                    ref, index = (e_2low, e_2high)[far], ()
                else:
                    ref, index = (e_0, e_1, None, e_3)[j], (far,)
                re, im = ref[(*index, 0)], ref[(*index, 1)]
                for part, block in enumerate((re, im, re + im)):
                    l_hi[part, at, :], l_lo[part, at, :] = split(block)

    dims = ((0,), (0,))
    l_re, l_im, l_sum = [(l_hi[part], l_lo[part]) for part in range(3)]
    re, im = [jnp.concatenate([b_ref[r, 0, part] for r in range(8)], axis=0) for part in range(2)]
    first, second = dot3(split(re), l_re, dims), dot3(split(im), l_im, dims)
    out_ref[0, 0] = first + second
    out_ref[0, 1] = dot3(split(re - im), l_sum, dims) - first + second


def update_kernel(own, other, *refs):
    x, y, zh = (lax.axis_index(name) for name in ("x", "y", "zh"))
    a_refs, (out_ref, m_hi, m_lo) = refs[:-3], refs[-3:]
    b, a = own.shape[2:]
    wide = a_refs[0].shape[-1]
    dims = ((1,), (0,))

    for level in range(2):
        for part in range(2):
            turned = other[level, part]
            turned = jnp.concatenate([turned[:, a // 2 :], turned[:, : a // 2]], axis=1)
            m_hi[level, part], m_lo[level, part] = split(own[level, part] + turned)

    def beside(p, q):
        return jnp.concatenate([p, q], axis=1)

    for j in range(4):
        sides = []
        for level in range(2):
            (rh, rl), (ih, il) = [
                split(jnp.concatenate([ref[level, part] for ref in a_refs[2 * j : 2 * j + 2]], axis=0))
                for part in range(2)
            ]
            sides.append(((beside(rh, ih), beside(rl, il)), (beside(-ih, rh), beside(-il, rl))))
        at = lax.rem(x + j + 4 - y, 4)
        for half_at in range(2):
            rows = slice(half_at * (b // 2), (half_at + 1) * (b // 2))
            total = None
            for level in range(2):
                for part in range(2):
                    left = m_hi[level, part, rows, :], m_lo[level, part, rows, :]
                    new = dot3(left, sides[level][part], dims)
                    total = new if total is None else total + new
            to = lax.rem(half_at + zh, 2)
            out_ref[at, to, 0] = total[:, :wide]
            out_ref[at, to, 1] = total[:, wide:]


def cost(flops, *values, scale=1):
    size = sum(v.dtype.itemsize * v.size for v in values)
    return pl.CostEstimate(flops=int(scale * flops), bytes_accessed=size, transcendentals=0)


def whole(n):
    return [pl.BlockSpec(memory_space=pltpu.VMEM)] * n


def mixed_partial(envs, sites):
    _, levels, _, depth, b = sites.shape
    a = envs[0].shape[-1]
    out = jax.ShapeDtypeStruct((levels, 2, 2 * b, a), F32)
    return pl.pallas_call(
        mixed_kernel,
        grid=(levels, 2),
        out_shape=out,
        in_specs=whole(len(envs))
        + [pl.BlockSpec((8, 1, 2, depth, b), lambda level, i: (i, level, 0, 0, 0))],
        out_specs=pl.BlockSpec((1, 2, b, a), lambda level, i: (level, 0, i, 0)),
        scratch_shapes=[pltpu.VMEM((3, 8 * depth, a), BF16)] * 2,
        compiler_params=pltpu.CompilerParams(vmem_limit_bytes=MIXED_VMEM),
        cost_estimate=cost(2 * 3 * 3 * levels * 8 * depth * 2 * b * a, out, sites, scale=MIXED_COST),
    )(*envs, sites)


def update_partial(shares, sites):
    levels, _, b, a = shares[0].shape
    c = sites[0].shape[-1]
    out = jax.ShapeDtypeStruct((4, 2, 2, b // 2, c), F32)
    operands = (*shares, *sites)
    return pl.pallas_call(
        update_kernel,
        out_shape=out,
        in_specs=whole(len(operands)),
        out_specs=pl.BlockSpec(memory_space=pltpu.VMEM),
        scratch_shapes=[pltpu.VMEM((levels, 2, b, a), BF16)] * 2,
        compiler_params=pltpu.CompilerParams(vmem_limit_bytes=VMEM),
        cost_estimate=cost(2 * 3 * 4 * levels * b * a * 4 * c, out, *operands, scale=COST),
    )(*operands)


def half(value, index, axis):
    size = value.shape[axis] // 2
    return lax.dynamic_slice_in_dim(value, index * size, size, axis)


def first_step(parts):
    return [move(parts[2, 0], "y", 1), move(parts[2, 1], "y", -1)]


def second_step(parts, came):
    up = move(jnp.stack([parts[1, 0] + came[0], parts[1, 1]]), "y", 1)
    down = move(jnp.stack([parts[3, 0], parts[3, 1] + came[1]]), "y", -1)
    return [up, down]


def to_place(mine, far, same):
    axes = ("zh", "zl")
    near = lax.ppermute(far, axes, [(1, 2), (2, 1)])
    got = lax.ppermute(jnp.where(same, far, mine), axes, [(0, 2), (1, 0), (2, 3), (3, 1)])
    return jnp.where(same, mine, near) + got


def local(environment, initial_site, compressed_site):
    zh, x, zl, y, core = (lax.axis_index(name) for name in PARTS)
    tie = lax.optimization_barrier

    comp = lax.all_gather(compressed_site, ("zh", "zl", "y"), axis=0)

    rows_other = move(half(environment, 1 - core, 1), "core", 1)
    env = jnp.concatenate([half(environment, core, 1), rows_other], axis=2)
    width = initial_site.shape[3] // 4
    cols_mine = half(initial_site, core, 3)
    cols_other = move(half(initial_site, 1 - core, 3), "core", 1)
    p_0, q_0 = [
        [v[..., i * width : (i + 1) * width] for v in (cols_mine, cols_other)] for i in range(2)
    ]

    env_far = move(env, "zh", 1)
    p_1 = [move(v, "x", -1) for v in p_0]
    p_3 = [move(v, "x", 1) for v in p_0]
    env, env_far, *more = tie((env, env_far, *p_1, *p_3, *q_0))
    p_1, p_3, q_0 = more[:2], more[2:4], more[4:]
    e_0 = jnp.stack([env, env_far])
    e_1 = move(e_0, "x", -1)
    e_3 = move(e_0, "x", 1)
    e_1, e_3, *more = tie((e_1, e_3, *p_1, *p_3))
    p_1, p_3 = more[:2], more[2:]
    e_2low = move(e_1[0], "x", -1)
    e_2high = move(e_3[1], "x", 1)
    p_2 = [move(p_1[0], "x", -1), move(p_3[1], "x", 1)]
    e_2low, e_2high, *q_0 = tie((e_2low, e_2high, *q_0))
    q_own = [move(q_0[0], "x", -1), move(q_0[0], "x", 1)]

    share = mixed_partial([e_0, e_1, e_3, e_2low, e_2high], comp)
    share, *more = tie((share, *p_2, *q_own, *q_0))
    p_2, q_own, q_0 = more[:2], more[2:4], more[4:]
    other = move(share, "core", 1)
    q_other = [move(q_0[1], "x", -1), move(q_0[1], "x", 1)]

    parts_0 = update_partial([share, other], [*p_0, *p_1, *p_2, *p_3])
    came_0 = first_step(parts_0)
    *q_own, q_other[0], q_other[1], parts_0 = tie((*q_own, *q_other, parts_0))
    q_1, q_3 = zip(q_own, q_other)
    q_2 = [move(q_own[0], "x", -1), move(q_other[1], "x", 1)]
    came_0 = second_step(parts_0, came_0)
    parts_1 = update_partial([share, other], [*q_0, *q_1, *q_2, *q_3])
    came_1 = first_step(parts_1)
    parts_1, *came = tie((parts_1, *came_0, *came_1))
    came_0, came_1 = came[:2], came[2:]
    came_1 = second_step(parts_1, came_1)

    results = []
    for parts, came in ((parts_0, came_0), (parts_1, came_1)):
        mine, far = parts[0] + came[0] + came[1]
        results.append(to_place(mine, far, zl == zh))
    return jnp.concatenate(results, axis=2)


def solution(mesh):
    names = tuple(PARTS)
    parts = Mesh(mesh.devices.reshape(tuple(PARTS.values())), names)
    row, col = names[:2], names[2:]
    return jax.shard_map(
        local,
        mesh=parts,
        in_specs=(P(None, row, col), P(None, None, col, row), P(None, None, col, row)),
        out_specs=P(None, row, col),
        check_vma=False,
    )
```

```python
import functools

import jax
import jax.numpy as jnp
from jax import lax
from jax.experimental import pallas as pl
from jax.experimental.pallas import tpu as pltpu
from jax.sharding import Mesh, PartitionSpec as P

PARTS = {"zh": 2, "x": 4, "zl": 2, "y": 4, "core": 2}
F32 = jnp.float32
BF16 = jnp.bfloat16
COST = 0.02
MIXED_COST = 0.02
VMEM = 24 * 1024 * 1024
MIXED_VMEM = 40 * 1024 * 1024


def move(value, axis, step):
    n = PARTS[axis]
    return lax.ppermute(value, axis, [(i, (i + step) % n) for i in range(n)])


def split(value):
    high = value.astype(BF16)
    return high, (value - high.astype(F32)).astype(BF16)


def dot3(left, right, dims):
    (lh, ll), (rh, rl) = left, right

    def one(a, b):
        return lax.dot_general(a, b, (dims, ((), ())), preferred_element_type=F32)

    return one(lh, rh) + (one(lh, rl) + one(ll, rh))


def mixed_kernel(e_0, e_1, e_3, e_2low, e_2high, b_ref, out_ref, l_hi, l_lo):
    zh, x = lax.axis_index("zh"), lax.axis_index("x")
    depth = e_0.shape[2]

    @pl.when((pl.program_id(0) == 0) & (pl.program_id(1) == 0))
    def _():
        for far in range(2):
            for j in range(4):
                row = 4 * lax.rem(zh + far, 2) + lax.rem(x + j, 4)
                at = pl.ds(pl.multiple_of(row * depth, depth), depth)
                if j == 2:
                    ref, index = (e_2low, e_2high)[far], ()
                else:
                    ref, index = (e_0, e_1, None, e_3)[j], (far,)
                re, im = ref[(*index, 0)], ref[(*index, 1)]
                for part, block in enumerate((re, im, re + im)):
                    l_hi[part, at, :], l_lo[part, at, :] = split(block)

    dims = ((0,), (0,))
    l_re, l_im, l_sum = [(l_hi[part], l_lo[part]) for part in range(3)]
    re, im = [jnp.concatenate([b_ref[r, 0, part] for r in range(8)], axis=0) for part in range(2)]
    first, second = dot3(split(re), l_re, dims), dot3(split(im), l_im, dims)
    out_ref[0, 0] = first + second
    out_ref[0, 1] = dot3(split(re - im), l_sum, dims) - first + second


def blocks(m_hi, m_lo, a_refs, from_x, out_ref):
    x, y, zh = (lax.axis_index(name) for name in ("x", "y", "zh"))
    b = m_hi.shape[2]
    wide = a_refs[0].shape[-1]
    dims = ((1,), (0,))

    def beside(p, q):
        return jnp.concatenate([p, q], axis=1)

    for n, j in enumerate(from_x):
        sides = []
        for level in range(2):
            (rh, rl), (ih, il) = [
                split(jnp.concatenate([ref[level, part] for ref in a_refs[2 * n : 2 * n + 2]], axis=0))
                for part in range(2)
            ]
            sides.append(((beside(rh, ih), beside(rl, il)), (beside(-ih, rh), beside(-il, rl))))
        at = lax.rem(x + j + 4 - y, 4)
        for half_at in range(2):
            rows = slice(half_at * (b // 2), (half_at + 1) * (b // 2))
            total = None
            for level in range(2):
                for part in range(2):
                    left = m_hi[level, part, rows, :], m_lo[level, part, rows, :]
                    new = dot3(left, sides[level][part], dims)
                    total = new if total is None else total + new
            to = lax.rem(half_at + zh, 2)
            out_ref[at, to, 0] = total[:, :wide]
            out_ref[at, to, 1] = total[:, wide:]


def first_kernel(own, other, *refs):
    a_refs, (out_ref, m_hi, m_lo) = refs[:-3], refs[-3:]
    a = own.shape[-1]
    for level in range(2):
        for part in range(2):
            turned = other[level, part]
            turned = jnp.concatenate([turned[:, a // 2 :], turned[:, : a // 2]], axis=1)
            m_hi[level, part], m_lo[level, part] = split(own[level, part] + turned)
    blocks(m_hi, m_lo, a_refs, range(4), out_ref)


def most_kernel(m_hi, m_lo, *refs):
    blocks(m_hi, m_lo, refs[:-1], (0, 1, 3), refs[-1])


def last_kernel(m_hi, m_lo, mine, theirs, so_far, out_ref):
    del so_far
    blocks(m_hi, m_lo, (mine, theirs), (2,), out_ref)


def cost(flops, *values, scale=1):
    size = sum(v.dtype.itemsize * v.size for v in values)
    return pl.CostEstimate(flops=int(scale * flops), bytes_accessed=size, transcendentals=0)


def whole(n):
    return [pl.BlockSpec(memory_space=pltpu.VMEM)] * n


def mixed_partial(envs, sites):
    _, levels, _, depth, b = sites.shape
    a = envs[0].shape[-1]
    out = jax.ShapeDtypeStruct((levels, 2, 2 * b, a), F32)
    return pl.pallas_call(
        mixed_kernel,
        grid=(levels, 2),
        out_shape=out,
        in_specs=whole(len(envs))
        + [pl.BlockSpec((8, 1, 2, depth, b), lambda level, i: (i, level, 0, 0, 0))],
        out_specs=pl.BlockSpec((1, 2, b, a), lambda level, i: (level, 0, i, 0)),
        scratch_shapes=[pltpu.VMEM((3, 8 * depth, a), BF16)] * 2,
        compiler_params=pltpu.CompilerParams(vmem_limit_bytes=MIXED_VMEM),
        cost_estimate=cost(2 * 3 * 3 * levels * 8 * depth * 2 * b * a, out, sites, scale=MIXED_COST),
    )(*envs, sites)


def update_partial(kernel, mixed, sites, so_far=None):
    levels, _, b, a = mixed[0].shape
    c = sites[0].shape[-1]
    out = [jax.ShapeDtypeStruct((4, 2, 2, b // 2, c), F32)]
    if kernel is first_kernel:
        out += [jax.ShapeDtypeStruct(mixed[0].shape, BF16)] * 2
    operands = (*mixed, *sites) if so_far is None else (*mixed, *sites, so_far)
    return pl.pallas_call(
        kernel,
        out_shape=out,
        in_specs=whole(len(operands)),
        out_specs=whole(len(out)),
        input_output_aliases={} if so_far is None else {len(operands) - 1: 0},
        compiler_params=pltpu.CompilerParams(vmem_limit_bytes=VMEM),
        cost_estimate=cost(3 * levels * b * a * len(sites) * 4 * c, *out, *operands, scale=COST),
    )(*operands)


def half(value, index, axis):
    size = value.shape[axis] // 2
    return lax.dynamic_slice_in_dim(value, index * size, size, axis)


def first_step(parts):
    return [move(parts[2, 0], "y", 1), move(parts[2, 1], "y", -1)]


def second_step(parts, came):
    up = move(jnp.stack([parts[1, 0] + came[0], parts[1, 1]]), "y", 1)
    down = move(jnp.stack([parts[3, 0], parts[3, 1] + came[1]]), "y", -1)
    return [up, down]


def to_place(mine, far, same):
    axes = ("zh", "zl")
    near = lax.ppermute(far, axes, [(1, 2), (2, 1)])
    got = lax.ppermute(jnp.where(same, far, mine), axes, [(0, 2), (1, 0), (2, 3), (3, 1)])
    return jnp.where(same, mine, near) + got


def round_ring(mine, far, same):
    axes = ("zh", "zl")
    across = lax.ppermute(far, axes, [(0, 3), (3, 0), (1, 2), (2, 1)])
    got = lax.ppermute(jnp.where(same, across, mine), axes, [(0, 1), (3, 2), (1, 0), (2, 3)])
    return jnp.where(same, mine, across) + got


def local(environment, initial_site, compressed_site):
    zh, x, zl, y, core = (lax.axis_index(name) for name in PARTS)
    tie = lax.optimization_barrier

    comp = lax.all_gather(compressed_site, ("zh", "zl", "y"), axis=0)

    rows_other = move(half(environment, 1 - core, 1), "core", 1)
    env = jnp.concatenate([half(environment, core, 1), rows_other], axis=2)
    width = initial_site.shape[3] // 4
    cols_mine = half(initial_site, core, 3)
    cols_other = move(half(initial_site, 1 - core, 3), "core", 1)
    p_0, q_0 = [
        [v[..., i * width : (i + 1) * width] for v in (cols_mine, cols_other)] for i in range(2)
    ]

    env_far = move(env, "zh", 1)
    p_1 = [move(v, "x", -1) for v in p_0]
    p_3 = [move(v, "x", 1) for v in p_0]
    env, env_far, *more = tie((env, env_far, *p_1, *p_3, *q_0))
    p_1, p_3, q_0 = more[:2], more[2:4], more[4:]
    e_0 = jnp.stack([env, env_far])
    e_1 = move(e_0, "x", -1)
    e_3 = move(e_0, "x", 1)
    e_1, e_3, *more = tie((e_1, e_3, *p_1, *p_3))
    p_1, p_3 = more[:2], more[2:]
    e_2low = move(e_1[0], "x", -1)
    e_2high = move(e_3[1], "x", 1)
    p_2 = [move(p_1[0], "x", -1), move(p_3[1], "x", 1)]
    e_2low, e_2high, *q_0 = tie((e_2low, e_2high, *q_0))
    q_own = [move(q_0[0], "x", -1), move(q_0[0], "x", 1)]

    share = mixed_partial([e_0, e_1, e_3, e_2low, e_2high], comp)
    share, *more = tie((share, *p_2, *q_own, *q_0))
    p_2, q_own, q_0 = more[:2], more[2:4], more[4:]
    other = move(share, "core", 1)
    q_other = [move(q_0[1], "x", -1), move(q_0[1], "x", 1)]

    parts_0, *mixed = update_partial(first_kernel, [share, other], [*p_0, *p_1, *p_2, *p_3])
    came_0 = first_step(parts_0)
    *q_own, q_other[0], q_other[1], parts_0 = tie((*q_own, *q_other, parts_0))
    q_1, q_3 = zip(q_own, q_other)
    q_2 = [move(q_own[0], "x", -1), move(q_other[1], "x", 1)]
    [parts_1] = update_partial(most_kernel, mixed, [*q_0, *q_1, *q_3])
    parts_1, *came_0 = tie((parts_1, *came_0))
    came_0 = second_step(parts_0, came_0)
    [parts_1] = update_partial(last_kernel, mixed, q_2, parts_1)
    came_1 = first_step(parts_1)
    parts_1, *came_0 = tie((parts_1, *came_0))
    result_0 = round_ring(*(parts_0[0] + came_0[0] + came_0[1]), zl == zh)
    came_1 = second_step(parts_1, came_1)
    results = [result_0, to_place(*(parts_1[0] + came_1[0] + came_1[1]), zl == zh)]
    return jnp.concatenate(results, axis=2)


def solution(mesh):
    names = tuple(PARTS)
    parts = Mesh(mesh.devices.reshape(tuple(PARTS.values())), names)
    row, col = names[:2], names[2:]
    return jax.shard_map(
        local,
        mesh=parts,
        in_specs=(P(None, row, col), P(None, None, col, row), P(None, None, col, row)),
        out_specs=P(None, row, col),
        check_vma=False,
    )
```

```python
import functools

import jax
import jax.numpy as jnp
from jax import lax
from jax.experimental import pallas as pl
from jax.experimental.pallas import tpu as pltpu
from jax.sharding import Mesh, PartitionSpec as P

PARTS = {"zh": 2, "x": 4, "zl": 2, "y": 4, "core": 2}
F32 = jnp.float32
BF16 = jnp.bfloat16
COST = 0.02
MIXED_COST = 0.02
VMEM = 24 * 1024 * 1024
MIXED_VMEM = 40 * 1024 * 1024


def move(value, axis, step):
    n = PARTS[axis]
    return lax.ppermute(value, axis, [(i, (i + step) % n) for i in range(n)])


def split(value):
    high = value.astype(BF16)
    return high, (value - high.astype(F32)).astype(BF16)


def dot3(left, right, dims):
    (lh, ll), (rh, rl) = left, right

    def one(a, b):
        return lax.dot_general(a, b, (dims, ((), ())), preferred_element_type=F32)

    return one(lh, rh) + (one(lh, rl) + one(ll, rh))


def mixed_kernel(e_0, e_1, e_3, e_2low, e_2high, b_ref, out_ref, l_hi, l_lo):
    zh, x = lax.axis_index("zh"), lax.axis_index("x")
    depth = e_0.shape[2]

    @pl.when((pl.program_id(0) == 0) & (pl.program_id(1) == 0))
    def _():
        for far in range(2):
            for j in range(4):
                row = 4 * lax.rem(zh + far, 2) + lax.rem(x + j, 4)
                at = pl.ds(pl.multiple_of(row * depth, depth), depth)
                if j == 2:
                    ref, index = (e_2low, e_2high)[far], ()
                else:
                    ref, index = (e_0, e_1, None, e_3)[j], (far,)
                re, im = ref[(*index, 0)], ref[(*index, 1)]
                for part, block in enumerate((re, im, re + im)):
                    l_hi[part, at, :], l_lo[part, at, :] = split(block)

    dims = ((0,), (0,))
    l_re, l_im, l_sum = [(l_hi[part], l_lo[part]) for part in range(3)]
    re, im = [jnp.concatenate([b_ref[r, 0, part] for r in range(8)], axis=0) for part in range(2)]
    first, second = dot3(split(re), l_re, dims), dot3(split(im), l_im, dims)
    out_ref[0, 0] = first + second
    out_ref[0, 1] = dot3(split(re - im), l_sum, dims) - first + second


def blocks(m_hi, m_lo, a_refs, from_x, out_ref):
    x, y, zh = (lax.axis_index(name) for name in ("x", "y", "zh"))
    b = m_hi.shape[2]
    wide = a_refs[0].shape[-1]
    dims = ((1,), (0,))

    def beside(p, q):
        return jnp.concatenate([p, q], axis=1)

    for n, j in enumerate(from_x):
        sides = []
        for level in range(2):
            (rh, rl), (ih, il) = [
                split(jnp.concatenate([ref[level, part] for ref in a_refs[2 * n : 2 * n + 2]], axis=0))
                for part in range(2)
            ]
            sides.append(((beside(rh, ih), beside(rl, il)), (beside(-ih, rh), beside(-il, rl))))
        at = lax.rem(x + j + 4 - y, 4)
        for half_at in range(2):
            rows = slice(half_at * (b // 2), (half_at + 1) * (b // 2))
            total = None
            for level in range(2):
                for part in range(2):
                    left = m_hi[level, part, rows, :], m_lo[level, part, rows, :]
                    new = dot3(left, sides[level][part], dims)
                    total = new if total is None else total + new
            to = lax.rem(half_at + zh, 2)
            out_ref[at, to, 0] = total[:, :wide]
            out_ref[at, to, 1] = total[:, wide:]


def first_kernel(own, other, *refs):
    a_refs, (out_ref, m_hi, m_lo) = refs[:-3], refs[-3:]
    a = own.shape[-1]
    for level in range(2):
        for part in range(2):
            turned = other[level, part]
            turned = jnp.concatenate([turned[:, a // 2 :], turned[:, : a // 2]], axis=1)
            m_hi[level, part], m_lo[level, part] = split(own[level, part] + turned)
    blocks(m_hi, m_lo, a_refs, range(4), out_ref)


def most_kernel(m_hi, m_lo, *refs):
    blocks(m_hi, m_lo, refs[:-1], (0, 1, 3), refs[-1])


def last_kernel(m_hi, m_lo, mine, theirs, so_far, out_ref):
    del so_far
    blocks(m_hi, m_lo, (mine, theirs), (2,), out_ref)


def cost(flops, *values, scale=1):
    size = sum(v.dtype.itemsize * v.size for v in values)
    return pl.CostEstimate(flops=int(scale * flops), bytes_accessed=size, transcendentals=0)


def whole(n):
    return [pl.BlockSpec(memory_space=pltpu.VMEM)] * n


def mixed_partial(envs, sites):
    _, levels, _, depth, b = sites.shape
    a = envs[0].shape[-1]
    out = jax.ShapeDtypeStruct((levels, 2, 2 * b, a), F32)
    return pl.pallas_call(
        mixed_kernel,
        grid=(levels, 2),
        out_shape=out,
        in_specs=whole(len(envs))
        + [pl.BlockSpec((8, 1, 2, depth, b), lambda level, i: (i, level, 0, 0, 0))],
        out_specs=pl.BlockSpec((1, 2, b, a), lambda level, i: (level, 0, i, 0)),
        scratch_shapes=[pltpu.VMEM((3, 8 * depth, a), BF16)] * 2,
        compiler_params=pltpu.CompilerParams(vmem_limit_bytes=MIXED_VMEM),
        cost_estimate=cost(2 * 3 * 3 * levels * 8 * depth * 2 * b * a, out, sites, scale=MIXED_COST),
    )(*envs, sites)


def update_partial(kernel, mixed, sites, so_far=None):
    levels, _, b, a = mixed[0].shape
    c = sites[0].shape[-1]
    out = [jax.ShapeDtypeStruct((4, 2, 2, b // 2, c), F32)]
    if kernel is first_kernel:
        out += [jax.ShapeDtypeStruct(mixed[0].shape, BF16)] * 2
    operands = (*mixed, *sites) if so_far is None else (*mixed, *sites, so_far)
    return pl.pallas_call(
        kernel,
        out_shape=out,
        in_specs=whole(len(operands)),
        out_specs=whole(len(out)),
        input_output_aliases={} if so_far is None else {len(operands) - 1: 0},
        compiler_params=pltpu.CompilerParams(vmem_limit_bytes=VMEM),
        cost_estimate=cost(3 * levels * b * a * len(sites) * 4 * c, *out, *operands, scale=COST),
    )(*operands)


def half(value, index, axis):
    size = value.shape[axis] // 2
    return lax.dynamic_slice_in_dim(value, index * size, size, axis)


def first_step(parts):
    return [move(parts[2, 0], "y", 1), move(parts[2, 1], "y", -1)]


def second_step(parts, came):
    up = move(jnp.stack([parts[1, 0] + came[0], parts[1, 1]]), "y", 1)
    down = move(jnp.stack([parts[3, 0], parts[3, 1] + came[1]]), "y", -1)
    return [up, down]


def to_place(mine, far, same):
    axes = ("zh", "zl")
    near = lax.ppermute(far, axes, [(1, 2), (2, 1)])
    got = lax.ppermute(jnp.where(same, far, mine), axes, [(0, 2), (1, 0), (2, 3), (3, 1)])
    return jnp.where(same, mine, near) + got


def round_ring(mine, far, same):
    axes = ("zh", "zl")
    across = lax.ppermute(far, axes, [(0, 3), (3, 0), (1, 2), (2, 1)])
    got = lax.ppermute(jnp.where(same, across, mine), axes, [(0, 1), (3, 2), (1, 0), (2, 3)])
    return jnp.where(same, mine, across) + got


def local(environment, initial_site, compressed_site):
    zh, x, zl, y, core = (lax.axis_index(name) for name in PARTS)
    tie = lax.optimization_barrier

    comp = lax.all_gather(compressed_site, ("zh", "zl", "y"), axis=0)

    rows_other = move(half(environment, 1 - core, 1), "core", 1)
    env = jnp.concatenate([half(environment, core, 1), rows_other], axis=2)
    width = initial_site.shape[3] // 4
    cols_mine = half(initial_site, core, 3)
    cols_other = move(half(initial_site, 1 - core, 3), "core", 1)
    p_0, q_0 = [
        [v[..., i * width : (i + 1) * width] for v in (cols_mine, cols_other)] for i in range(2)
    ]

    env_far = move(env, "zh", 1)
    p_1 = [move(v, "x", -1) for v in p_0]
    p_3 = [move(v, "x", 1) for v in p_0]
    env, env_far, *more = tie((env, env_far, *p_1, *p_3, *q_0))
    p_1, p_3, q_0 = more[:2], more[2:4], more[4:]
    e_0 = jnp.stack([env, env_far])
    e_1 = move(e_0, "x", -1)
    e_3 = move(e_0, "x", 1)
    e_1, e_3, *more = tie((e_1, e_3, *p_1, *p_3))
    p_1, p_3 = more[:2], more[2:]
    e_2low = move(e_1[0], "x", -1)
    e_2high = move(e_3[1], "x", 1)
    p_2 = [move(p_1[0], "x", -1), move(p_3[1], "x", 1)]
    e_2low, e_2high, *q_0 = tie((e_2low, e_2high, *q_0))
    q_own = [move(q_0[0], "x", -1), move(q_0[0], "x", 1)]

    share = mixed_partial([e_0, e_1, e_3, e_2low, e_2high], comp)
    share, *more = tie((share, *p_2, *q_own, *q_0))
    p_2, q_own, q_0 = more[:2], more[2:4], more[4:]
    other = move(share, "core", 1)
    q_other = [move(q_0[1], "x", -1), move(q_0[1], "x", 1)]

    parts_0, *mixed = update_partial(first_kernel, [share, other], [*p_0, *p_1, *p_2, *p_3])
    came_0 = first_step(parts_0)
    *q_own, q_other[0], q_other[1], parts_0 = tie((*q_own, *q_other, parts_0))
    q_1, q_3 = zip(q_own, q_other)
    q_2 = [move(q_own[0], "x", -1), move(q_other[1], "x", 1)]
    came_0 = second_step(parts_0, came_0)
    [parts_1] = update_partial(most_kernel, mixed, [*q_0, *q_1, *q_3])
    parts_1, *q_2 = tie((parts_1, *q_2))
    [parts_1] = update_partial(last_kernel, mixed, q_2, parts_1)
    came_1 = first_step(parts_1)
    parts_1, *came_0 = tie((parts_1, *came_0))
    result_0 = round_ring(*(parts_0[0] + came_0[0] + came_0[1]), zl == zh)
    came_1 = second_step(parts_1, came_1)
    results = [result_0, to_place(*(parts_1[0] + came_1[0] + came_1[1]), zl == zh)]
    return jnp.concatenate(results, axis=2)


def solution(mesh):
    names = tuple(PARTS)
    parts = Mesh(mesh.devices.reshape(tuple(PARTS.values())), names)
    row, col = names[:2], names[2:]
    return jax.shard_map(
        local,
        mesh=parts,
        in_specs=(P(None, row, col), P(None, None, col, row), P(None, None, col, row)),
        out_specs=P(None, row, col),
        check_vma=False,
    )
```

```python
import functools

import jax
import jax.numpy as jnp
from jax import lax
from jax.experimental import pallas as pl
from jax.experimental.pallas import tpu as pltpu
from jax.sharding import Mesh, PartitionSpec as P

PARTS = {"zh": 2, "x": 4, "zl": 2, "y": 4, "core": 2}
F32 = jnp.float32
BF16 = jnp.bfloat16
COST = 0.02
MIXED_COST = 0.02
VMEM = 24 * 1024 * 1024
MIXED_VMEM = 40 * 1024 * 1024


def move(value, axis, step):
    n = PARTS[axis]
    return lax.ppermute(value, axis, [(i, (i + step) % n) for i in range(n)])


def split(value):
    high = value.astype(BF16)
    return high, (value - high.astype(F32)).astype(BF16)


def dot3(left, right, dims):
    (lh, ll), (rh, rl) = left, right

    def one(a, b):
        return lax.dot_general(a, b, (dims, ((), ())), preferred_element_type=F32)

    return one(lh, rh) + (one(lh, rl) + one(ll, rh))


def mixed_kernel(e_0, e_1, e_3, e_2low, e_2high, b_ref, out_ref, l_hi, l_lo):
    zh, x = lax.axis_index("zh"), lax.axis_index("x")
    depth = e_0.shape[2]

    @pl.when((pl.program_id(0) == 0) & (pl.program_id(1) == 0))
    def _():
        for far in range(2):
            for j in range(4):
                row = 4 * lax.rem(zh + far, 2) + lax.rem(x + j, 4)
                at = pl.ds(pl.multiple_of(row * depth, depth), depth)
                if j == 2:
                    ref, index = (e_2low, e_2high)[far], ()
                else:
                    ref, index = (e_0, e_1, None, e_3)[j], (far,)
                re, im = ref[(*index, 0)], ref[(*index, 1)]
                for part, block in enumerate((re, im, re + im)):
                    l_hi[part, at, :], l_lo[part, at, :] = split(block)

    dims = ((0,), (0,))
    l_re, l_im, l_sum = [(l_hi[part], l_lo[part]) for part in range(3)]
    re, im = [jnp.concatenate([b_ref[r, 0, part] for r in range(8)], axis=0) for part in range(2)]
    first, second = dot3(split(re), l_re, dims), dot3(split(im), l_im, dims)
    out_ref[0, 0] = first + second
    out_ref[0, 1] = dot3(split(re - im), l_sum, dims) - first + second


def blocks(m_hi, m_lo, a_refs, from_x, out_ref):
    x, y, zh = (lax.axis_index(name) for name in ("x", "y", "zh"))
    b = m_hi.shape[2]
    wide = a_refs[0].shape[-1]
    dims = ((1,), (0,))

    def beside(p, q):
        return jnp.concatenate([p, q], axis=1)

    for n, j in enumerate(from_x):
        sides = []
        for level in range(2):
            (rh, rl), (ih, il) = [
                split(jnp.concatenate([ref[level, part] for ref in a_refs[2 * n : 2 * n + 2]], axis=0))
                for part in range(2)
            ]
            sides.append(((beside(rh, ih), beside(rl, il)), (beside(-ih, rh), beside(-il, rl))))
        at = lax.rem(x + j + 4 - y, 4)
        for half_at in range(2):
            rows = slice(half_at * (b // 2), (half_at + 1) * (b // 2))
            total = None
            for level in range(2):
                for part in range(2):
                    left = m_hi[level, part, rows, :], m_lo[level, part, rows, :]
                    new = dot3(left, sides[level][part], dims)
                    total = new if total is None else total + new
            to = lax.rem(half_at + zh, 2)
            out_ref[at, to, 0] = total[:, :wide]
            out_ref[at, to, 1] = total[:, wide:]


def first_kernel(own, other, *refs):
    a_refs, (out_ref, m_hi, m_lo) = refs[:-3], refs[-3:]
    a = own.shape[-1]
    for level in range(2):
        for part in range(2):
            turned = other[level, part]
            turned = jnp.concatenate([turned[:, a // 2 :], turned[:, : a // 2]], axis=1)
            m_hi[level, part], m_lo[level, part] = split(own[level, part] + turned)
    blocks(m_hi, m_lo, a_refs, range(4), out_ref)


def most_kernel(m_hi, m_lo, *refs):
    blocks(m_hi, m_lo, refs[:-1], (0, 1, 3), refs[-1])


def last_kernel(m_hi, m_lo, mine, theirs, so_far, out_ref):
    del so_far
    blocks(m_hi, m_lo, (mine, theirs), (2,), out_ref)


def cost(flops, *values, scale=1):
    size = sum(v.dtype.itemsize * v.size for v in values)
    return pl.CostEstimate(flops=int(scale * flops), bytes_accessed=size, transcendentals=0)


def whole(n):
    return [pl.BlockSpec(memory_space=pltpu.VMEM)] * n


def mixed_partial(envs, sites):
    _, levels, _, depth, b = sites.shape
    a = envs[0].shape[-1]
    out = jax.ShapeDtypeStruct((levels, 2, 2 * b, a), F32)
    return pl.pallas_call(
        mixed_kernel,
        grid=(levels, 2),
        out_shape=out,
        in_specs=whole(len(envs))
        + [pl.BlockSpec((8, 1, 2, depth, b), lambda level, i: (i, level, 0, 0, 0))],
        out_specs=pl.BlockSpec((1, 2, b, a), lambda level, i: (level, 0, i, 0)),
        scratch_shapes=[pltpu.VMEM((3, 8 * depth, a), BF16)] * 2,
        compiler_params=pltpu.CompilerParams(vmem_limit_bytes=MIXED_VMEM),
        cost_estimate=cost(2 * 3 * 3 * levels * 8 * depth * 2 * b * a, out, sites, scale=MIXED_COST),
    )(*envs, sites)


def update_partial(kernel, mixed, sites, so_far=None):
    levels, _, b, a = mixed[0].shape
    c = sites[0].shape[-1]
    out = [jax.ShapeDtypeStruct((4, 2, 2, b // 2, c), F32)]
    if kernel is first_kernel:
        out += [jax.ShapeDtypeStruct(mixed[0].shape, BF16)] * 2
    operands = (*mixed, *sites) if so_far is None else (*mixed, *sites, so_far)
    return pl.pallas_call(
        kernel,
        out_shape=out,
        in_specs=whole(len(operands)),
        out_specs=whole(len(out)),
        input_output_aliases={} if so_far is None else {len(operands) - 1: 0},
        compiler_params=pltpu.CompilerParams(vmem_limit_bytes=VMEM),
        cost_estimate=cost(3 * levels * b * a * len(sites) * 4 * c, *out, *operands, scale=COST),
    )(*operands)


def half(value, index, axis):
    size = value.shape[axis] // 2
    return lax.dynamic_slice_in_dim(value, index * size, size, axis)


def first_step(parts):
    return [move(parts[2, 0], "y", 1), move(parts[2, 1], "y", -1)]


def second_step(parts, came):
    up = move(jnp.stack([parts[1, 0] + came[0], parts[1, 1]]), "y", 1)
    down = move(jnp.stack([parts[3, 0], parts[3, 1] + came[1]]), "y", -1)
    return [up, down]


def round_ring(mine, far, same):
    axes = ("zh", "zl")
    across = lax.ppermute(far, axes, [(0, 3), (3, 0), (1, 2), (2, 1)])
    got = lax.ppermute(jnp.where(same, across, mine), axes, [(0, 1), (3, 2), (1, 0), (2, 3)])
    return jnp.where(same, mine, across) + got


def local(environment, initial_site, compressed_site):
    zh, x, zl, y, core = (lax.axis_index(name) for name in PARTS)
    tie = lax.optimization_barrier

    comp = lax.all_gather(compressed_site, ("zh", "zl", "y"), axis=0)

    rows_other = move(half(environment, 1 - core, 1), "core", 1)
    env = jnp.concatenate([half(environment, core, 1), rows_other], axis=2)
    width = initial_site.shape[3] // 4
    cols_mine = half(initial_site, core, 3)
    cols_other = move(half(initial_site, 1 - core, 3), "core", 1)
    p_0, q_0 = [
        [v[..., i * width : (i + 1) * width] for v in (cols_mine, cols_other)] for i in range(2)
    ]

    env_far = move(env, "zh", 1)
    p_1 = [move(v, "x", -1) for v in p_0]
    p_3 = [move(v, "x", 1) for v in p_0]
    env, env_far, *more = tie((env, env_far, *p_1, *p_3, *q_0))
    p_1, p_3, q_0 = more[:2], more[2:4], more[4:]
    e_0 = jnp.stack([env, env_far])
    e_1 = move(e_0, "x", -1)
    e_3 = move(e_0, "x", 1)
    e_1, e_3, *more = tie((e_1, e_3, *p_1, *p_3))
    p_1, p_3 = more[:2], more[2:]
    e_2low = move(e_1[0], "x", -1)
    e_2high = move(e_3[1], "x", 1)
    p_2 = [move(p_1[0], "x", -1), move(p_3[1], "x", 1)]
    e_2low, e_2high, *q_0 = tie((e_2low, e_2high, *q_0))
    q_own = [move(q_0[0], "x", -1), move(q_0[0], "x", 1)]

    share = mixed_partial([e_0, e_1, e_3, e_2low, e_2high], comp)
    share, *more = tie((share, *p_2, *q_own, *q_0))
    p_2, q_own, q_0 = more[:2], more[2:4], more[4:]
    other = move(share, "core", 1)
    q_other = [move(q_0[1], "x", -1), move(q_0[1], "x", 1)]

    parts_0, *mixed = update_partial(first_kernel, [share, other], [*p_0, *p_1, *p_2, *p_3])
    came_0 = first_step(parts_0)
    *q_own, q_other[0], q_other[1], parts_0 = tie((*q_own, *q_other, parts_0))
    q_1, q_3 = zip(q_own, q_other)
    q_2 = [move(q_own[0], "x", -1), move(q_other[1], "x", 1)]
    came_0 = second_step(parts_0, came_0)
    [parts_1] = update_partial(most_kernel, mixed, [*q_0, *q_1, *q_3])
    parts_1, *q_2 = tie((parts_1, *q_2))
    [parts_1] = update_partial(last_kernel, mixed, q_2, parts_1)
    came_1 = first_step(parts_1)
    parts_1, *came_0 = tie((parts_1, *came_0))
    result_0 = round_ring(*(parts_0[0] + came_0[0] + came_0[1]), zl == zh)
    came_1 = second_step(parts_1, came_1)
    results = [result_0, round_ring(*(parts_1[0] + came_1[0] + came_1[1]), zl == zh)]
    return jnp.concatenate(results, axis=2)


def solution(mesh):
    names = tuple(PARTS)
    parts = Mesh(mesh.devices.reshape(tuple(PARTS.values())), names)
    row, col = names[:2], names[2:]
    return jax.shard_map(
        local,
        mesh=parts,
        in_specs=(P(None, row, col), P(None, None, col, row), P(None, None, col, row)),
        out_specs=P(None, row, col),
        check_vma=False,
    )
```
